32 devices in a mesh: group: 2 (over y), leaf: 8 (over z, x), rhs: 2 (over core).
Axes of the slice: x: 2, y: 2, z: 4, core: 2. Of those that a mesh axis runs over, the one named last changes fastest.
Arguments:
- iterate: float32 [128, 16384], P(('group', 'rhs'), 'leaf'), parts along dimension 0, may hold values from -6 to 6
- target: float32 [128, 16384], P(('group', 'rhs'), 'leaf'), parts along dimension 0
- coords: int32 [3, 32768], P(None, ('group', 'leaf')), parts along dimension 1, may hold values from 0 to 63
- tree_order: int32 [16, 2048], P(('group', 'leaf')), parts along dimension 0, may hold values from 0 to 2047, each once within a row
- leaf_basis: bfloat16 [32768, 256], P(('group', 'leaf')), parts along dimension 0, may hold values from -0.125 to 0.125
- transfer: bfloat16 [16, 2, 256, 256], P(('group', 'leaf')), parts along dimension 0, as said below
- coupling: bfloat16 [16, 3, 256, 256], P(('group', 'leaf')), parts along dimension 0, as said below
Outputs:
- direction: float32 [128, 16384], P(('group', 'rhs'), 'leaf'), parts along dimension 0
The draws below stay inside these ranges and needn't reach their ends.
There are 2 independent parts, one for each index of `group`. The reference program is written for one: setup_inputs(seed, part) draws one part's arguments, and reference() takes and returns one part's arrays. A program takes and returns all parts, laid end to end along the dimension named above; each array names one. Nothing has to cross between parts.
Inputs may be any that keep to these rules, and one draw needn't show every extreme that they name: transfer[j, k] is the same for all leaves j that share their level-k node (equal j // 2**k). coupling[j, k] is the same for all leaves j that share their level-k node (equal j // 2**k).
All inputs are finite; a program needn't handle non-finite values.
Results may differ from the reference program's by a relative error of at most 0.0016.
Values sent between devices are 32-bit elements; how exact they have to be, the bound alone decides.
A program may use at most 64 MiB of HBM per device.

```python
import math
import jax
import jax.numpy as jnp
from jax import lax

LEAF = 2048
RANK = 256
RHS = 64
LEAVES = 8
POINTS = 16384
LEVELS = 3
N_LEAF = 8


def level_table(key, levels_count, half_width, growth):
    leaf_ids = jnp.arange(LEAVES, dtype=jnp.int32)
    slabs = []
    for height in range(levels_count):
        level_key = jax.random.fold_in(key, height)
        level_width = half_width * growth ** height

        def one_leaf(leaf_id):
            node_key = jax.random.fold_in(level_key, jnp.right_shift(leaf_id, height))
            return jax.random.uniform(node_key, (RANK, RANK), jnp.float32, -level_width, level_width)
        slabs.append(jax.vmap(one_leaf)(leaf_ids))
    return jnp.stack(slabs, axis=1)


def draw_transfer(key, part):
    key = jax.random.fold_in(key, 5)
    half_width = (3.0 / (2 * RANK)) ** 0.5
    return level_table(key, LEVELS - 1, half_width, 1.0).astype(jnp.bfloat16)


def draw_coupling(key, part):
    key = jax.random.fold_in(key, 7)
    half_width = (3.0 / RANK) ** 0.5
    return level_table(key, LEVELS, half_width, 2.0 ** 0.5).astype(jnp.bfloat16)


def draw_target(key, part):
    key = jax.random.fold_in(key, 11)
    first_key, second_key = jax.random.split(key, 2)
    spots = jnp.arange(POINTS, dtype=jnp.float32) / POINTS
    row_scale = 0.6 * jnp.exp(math.log(3.0) * jax.random.uniform(second_key, (RHS, 1), jnp.float32))
    values = jax.random.normal(first_key, (RHS, POINTS), jnp.float32)
    envelope = 0.3 * jnp.exp(math.log(10.0) * spots)
    return values * envelope[None, :] * row_scale


def with_ends(array, key, smallest, top_value):
    longest = array.shape.index(max(array.shape))
    spots = []
    for shift in (0, 1):
        where = [jax.random.randint(jax.random.fold_in(key, axis), (), 0, length) for axis, length in enumerate(array.shape)]
        where[longest] = (where[longest] + shift) % array.shape[longest]
        spots.append(tuple(where))
    return array.at[spots[0]].set(smallest).at[spots[1]].set(top_value)


def block_scale(stream_key, shape, pieces, smallest, high):
    loudness = 1.0
    for axis_at, blocks in pieces:
        heights = jax.random.uniform(jax.random.fold_in(jax.random.fold_in(stream_key, 6), axis_at), (blocks,), jnp.float32, smallest / len(pieces), high / len(pieces))
        loudness = loudness * jnp.repeat(jnp.exp(heights), shape[axis_at] // blocks).reshape((-1,) + (1,) * (len(shape) - 1 - axis_at))
    return loudness


def gaussian(key, extent, deviation, most, shards=(), held_as=jnp.bfloat16):
    values = deviation * jax.random.normal(key, extent, jnp.float32)
    if shards:
        values = values * block_scale(key, extent, shards, -0.22, 0.18)
    return jnp.clip(values, -most, most).astype(held_as)


def setup_inputs(seed: int = 0, part: int = 0) -> dict:
    key_of = jax.random.split(jax.random.key(seed), 8)
    own_keys = jax.random.split(jax.random.fold_in(key_of[7], part), 8)
    iterate = gaussian(own_keys[0], (RHS, POINTS), 1.0, 6.0, ((0, 2), (1, 8)), jnp.float32)
    target = draw_target(jax.random.fold_in(jax.random.fold_in(key_of[7], part), 71), part)
    coords = with_ends(jax.random.randint(own_keys[2], (3, POINTS), 0, 64), jax.random.fold_in(own_keys[2], 1), 0, 63).astype(jnp.int32)
    tree_order = jax.vmap(lambda own: jax.random.permutation(own, LEAF))(jax.random.split(own_keys[3], LEAVES)).reshape((LEAVES, LEAF)).astype(jnp.int32)
    leaf_basis = gaussian(own_keys[4], (POINTS, RANK), LEAF ** -0.5, 0.125, ((0, 8),))
    transfer = draw_transfer(jax.random.fold_in(jax.random.fold_in(key_of[7], part), 71), part)
    coupling = draw_coupling(jax.random.fold_in(jax.random.fold_in(key_of[7], part), 71), part)
    return {"iterate": iterate, "target": target, "coords": coords, "tree_order": tree_order, "leaf_basis": leaf_basis, "transfer": transfer, "coupling": coupling}


def matern_block(left_coords, right_coords):
    squared = (left_coords[0][:, None] - right_coords[0][None, :]) ** 2
    squared = squared + (left_coords[1][:, None] - right_coords[1][None, :]) ** 2
    squared = squared + (left_coords[2][:, None] - right_coords[2][None, :]) ** 2
    scaled = jnp.sqrt(3.0 * squared) * 0.0625
    return (1.0 + scaled) * jnp.exp(-scaled)

def reference(iterate, target, coords, tree_order, leaf_basis, transfer, coupling):
    highest = lax.Precision.HIGHEST
    leaves = N_LEAF
    sendable = LEAF // leaves
    sources = jnp.arange(leaves, dtype=jnp.int32)[:, None] * LEAF + tree_order
    tree_index = sources.reshape(leaves, leaves, sendable).transpose(1, 0, 2).reshape(-1).astype(jnp.int32)
    tree_values = iterate[:, tree_index]
    tree_coords = coords[:, tree_index].astype(jnp.float32)
    values_by_leaf = tree_values.reshape(RHS, leaves, LEAF).transpose(1, 0, 2)
    coords_by_leaf = tree_coords.reshape(3, leaves, LEAF).transpose(1, 0, 2)

    def leaf_near(operands):
        values, points = operands
        kernel = matern_block(points, points)
        return 0.0625 * jnp.dot(values, kernel, precision=highest)
    nearby = lax.map(leaf_near, (values_by_leaf, coords_by_leaf))
    rounded = lax.optimization_barrier(values_by_leaf.astype(jnp.bfloat16)).astype(jnp.float32)
    basis_full = leaf_basis.astype(jnp.float32).reshape(leaves, LEAF, RANK)
    skeleton = [jnp.einsum('jrp,jpk->jrk', rounded, basis_full, precision=highest)]
    for height in range(LEVELS - 1):
        table = transfer[::2 ** height, height].astype(jnp.float32)
        lifted = jnp.einsum('mrk,mkl->mrl', skeleton[height], table, precision=highest)
        skeleton.append(lifted[0::2] + lifted[1::2])
    coupled = []
    for height in range(LEVELS):
        couplings = coupling[::2 ** height, height].astype(jnp.float32)
        nodes = skeleton[height]
        partner = nodes.reshape(-1, 2, RHS, RANK)[:, ::-1].reshape(nodes.shape)
        coupled.append(jnp.einsum('mrk,mkl->mrl', partner, couplings, precision=highest))
    downward = coupled[LEVELS - 1]
    for height in range(LEVELS - 2, -1, -1):
        table = transfer[::2 ** height, height].astype(jnp.float32)
        parents = jnp.repeat(downward, 2, axis=0)
        downward = coupled[height] + jnp.einsum('mrl,mkl->mrk', parents, table, precision=highest)
    down_rounded = lax.optimization_barrier(downward.astype(jnp.bfloat16)).astype(jnp.float32)
    far_field = jnp.einsum('jrk,jpk->jrp', down_rounded, basis_full, precision=highest)
    applied = (nearby + far_field).transpose(1, 0, 2).reshape(RHS, POINTS)
    placed = jnp.zeros_like(target).at[:, tree_index].set(applied)
    residual = target - placed
    power = lax.optimization_barrier(jnp.sum(residual * residual, axis=1, keepdims=True))
    return residual / jnp.sqrt(power / POINTS + 1e-06)
```

```python
import functools
import jax
import jax.numpy as jnp
from jax import lax
from jax.experimental import pallas as pl
from jax.experimental.pallas import tpu as pltpu
from jax.sharding import PartitionSpec as P

F32 = jnp.float32
BF16 = jnp.bfloat16
MESH = pl.DeviceIdType.MESH
ROWS_T = (((1,), (1,)), ((), ()))
COLS_T = (((0,), (0,)), ((), ()))


def far_first(t, n):
    if n == 2:
        return 1 - t
    return n // 2 + ((t + 1) // 2) * (1 - 2 * (t % 2))


def halves(x):
    high = x.astype(BF16)
    low = (x - high.astype(F32)).astype(BF16)
    return jnp.concatenate([high, low], axis=0)


def split_dot(x, right, dims):
    rows = x.shape[0]
    both = lax.dot_general(halves(x), right, dims, preferred_element_type=F32)
    return both[:rows] + both[rows:]


def fused(
    n, levels, eval_blocks,
    iterate, target, coords, order, basis, transfer, coupling,
    out,
    parts, coord_rows, onehot, send_values, send_coords, tree_values, tree_coords,
    left_feat, right_feat, left_t, kernel_k, skel_send, skel_recv, lift_send, lift_recv,
    applied, returned, placed, power_send, power_recv,
    c_ss, c_rs, v_ss, v_rs, s_ss, s_rs, l_ss, l_rs, b_ss, b_rs, p_ss, p_rs,
):
    rhs, width = iterate.shape
    share = width // n
    me = lax.axis_index("leaf")

    def peer(offset):
        return lax.rem(me + offset, n)

    def source(offset):
        return lax.rem(me + n - offset, n)

    def cols(index):
        return pl.ds(pl.multiple_of(index * share, share), share)

    barrier = pltpu.get_barrier_semaphore()
    for offset in range(1, n):
        pl.semaphore_signal(barrier, inc=1, device_id={"leaf": peer(offset)}, device_id_type=MESH)

    parts[0:2 * rhs, :] = halves(iterate[...])
    coord_rows[...] = jnp.zeros_like(coord_rows)
    coord_rows[0:3, :] = coords[...].astype(F32)
    parts[2 * rhs:2 * rhs + 16, :] = coord_rows[...].astype(BF16)

    def coord_copy(d):
        return pltpu.make_async_remote_copy(
            src_ref=send_coords.at[d], dst_ref=tree_coords.at[:, cols(me)],
            send_sem=c_ss.at[d], recv_sem=c_rs.at[d],
            device_id={"leaf": peer(d)}, device_id_type=MESH)

    def value_copy(d):
        return pltpu.make_async_remote_copy(
            src_ref=send_values.at[d], dst_ref=tree_values.at[:, cols(me)],
            send_sem=v_ss.at[d], recv_sem=v_rs.at[d],
            device_id={"leaf": peer(d)}, device_id_type=MESH)

    for t in range(n):
        d = far_first(t, n)
        where = cols(peer(d))
        spots = lax.broadcasted_iota(jnp.int32, (width, share), 0)
        chosen = (spots == order[:, where]).astype(F32).astype(BF16)
        onehot[:, where] = chosen
        moved = jnp.dot(parts[...], chosen, preferred_element_type=F32)
        if d:
            send_values[d] = moved[:rhs] + moved[rhs:2 * rhs]
            send_coords[d] = moved[2 * rhs:2 * rhs + 8]
            if t == 0:
                pl.semaphore_wait(barrier, n - 1)
            coord_copy(d).start()
        else:
            tree_values[:, where] = moved[:rhs] + moved[rhs:2 * rhs]
            tree_coords[:, where] = moved[2 * rhs:2 * rhs + 8]
    for t in range(n - 1):
        value_copy(far_first(t, n)).start()

    for d in range(1, n):
        coord_copy(d).wait_recv()
    xyz = tree_coords[0:3, :]
    norm = jnp.sum(xyz * xyz, axis=0, keepdims=True)
    norm_high = jnp.floor(norm * (1.0 / 256.0))
    norm_low = norm - 256.0 * norm_high
    left_feat[...] = jnp.zeros_like(left_feat)
    right_feat[...] = jnp.zeros_like(right_feat)
    left_feat[0:3, :] = xyz
    left_feat[3:4, :] = norm_low
    left_feat[4:5, :] = norm_high
    left_feat[5:6, :] = jnp.full_like(norm, 3.0 / 256.0)
    left_feat[6:7, :] = jnp.full_like(norm, 3.0)
    right_feat[0:3, :] = xyz * (-6.0 / 256.0)
    right_feat[3:4, :] = jnp.full_like(norm, 3.0 / 256.0)
    right_feat[4:5, :] = jnp.full_like(norm, 3.0)
    right_feat[5:6, :] = norm_low
    right_feat[6:7, :] = norm_high
    left_t[...] = left_feat[...].T.astype(BF16)

    rows_step = 256

    def matern_column(t):
        where = cols(peer(far_first(t, n)))
        right = right_feat[:, where].astype(BF16)

        @pl.loop(0, width // rows_step)
        def _(step):
            rows = pl.ds(pl.multiple_of(step * rows_step, rows_step), rows_step)
            q = jnp.dot(left_t[rows, :], right, preferred_element_type=F32)
            s = q * lax.rsqrt(jnp.maximum(q, 1e-30))
            kernel_k[rows, where] = ((1.0 + s) * jnp.exp2(s * (-1.4426950408889634))).astype(BF16)

    done = 0

    def matern_until(count):
        nonlocal done
        while done < min(count, n):
            matern_column(done)
            done += 1

    matern_until(eval_blocks[0])

    for d in range(1, n):
        value_copy(d).wait_recv()
    skeleton = jnp.dot(tree_values[...].astype(BF16), basis[...], preferred_element_type=F32)

    def tree_copy(send, recv, ss, rs, height):
        stride = 2 ** height
        partner = me + stride * (1 - 2 * lax.rem(me // stride, 2))
        return pltpu.make_async_remote_copy(
            src_ref=send.at[height], dst_ref=recv.at[height],
            send_sem=ss.at[height], recv_sem=rs.at[height],
            device_id={"leaf": partner}, device_id_type=MESH)

    coupled = []
    plain = (((1,), (0,)), ((), ()))
    for height in range(levels):
        last = height == levels - 1
        skel_copy = tree_copy(skel_send, skel_recv, s_ss, s_rs, height)
        skel_send[height] = skeleton
        skel_copy.start()
        if not last:
            lifted = split_dot(skeleton, transfer[0, height], plain)
            lift_send[height] = lifted
            lift_copy = tree_copy(lift_send, lift_recv, l_ss, l_rs, height)
            lift_copy.start()
        matern_until(eval_blocks[min(height + 1, len(eval_blocks) - 1)])
        if last:
            matern_until(n)
        skel_copy.wait_recv()
        coupled.append(split_dot(skel_recv[height], coupling[0, height], plain))
        if not last:
            lift_copy.wait_recv()
            skeleton = lifted + lift_recv[height]
    downward = coupled[-1]
    for height in range(levels - 2, -1, -1):
        downward = coupled[height] + split_dot(downward, transfer[0, height], ROWS_T)
    down = downward.astype(BF16)

    def back_copy(d):
        return pltpu.make_async_remote_copy(
            src_ref=applied.at[d], dst_ref=returned.at[:, cols(me)],
            send_sem=b_ss.at[d], recv_sem=b_rs.at[d],
            device_id={"leaf": peer(d)}, device_id_type=MESH)

    values = halves(tree_values[...])
    for t in range(n):
        d = far_first(t, n)
        where = cols(peer(d))
        near = jnp.dot(values, kernel_k[:, where], preferred_element_type=F32)
        far = lax.dot_general(down, basis[cols(peer(d)), :], ROWS_T, preferred_element_type=F32)
        total = 0.0625 * (near[:rhs] + near[rhs:]) + far
        if d:
            applied[d] = total
            back_copy(d).start()
        else:
            returned[:, where] = total

    def put_back(index):
        where = cols(index)
        return lax.dot_general(halves(returned[:, where]), onehot[:, where], ROWS_T,
                               preferred_element_type=F32)

    placed[...] = put_back(me)
    for t in range(n - 2, -1, -1):
        d = far_first(t, n)
        back_copy(d).wait_recv()
        placed[...] += put_back(source(d))
    residual = target[...] - (placed[:rhs] + placed[rhs:])
    power = jnp.sum(residual * residual, axis=1, keepdims=True)

    tall = jnp.broadcast_to(power, (rhs, 128))
    square = jnp.concatenate([tall] * (128 // rhs), axis=0)
    power_send[...] = square.T[0:8, :]

    def power_copy(d):
        return pltpu.make_async_remote_copy(
            src_ref=power_send, dst_ref=power_recv.at[d],
            send_sem=p_ss.at[d], recv_sem=p_rs.at[d],
            device_id={"leaf": peer(d)}, device_id_type=MESH)

    for t in range(n - 1):
        power_copy(far_first(t, n)).start()
    whole = power_send[...]
    for d in range(1, n):
        power_copy(d).wait_recv()
        whole = whole + power_recv[d]
    total_power = jnp.concatenate([whole] * 16, axis=0).T[0:rhs, 0:1]
    out[...] = residual * lax.rsqrt(total_power * (1.0 / (width * n)) + 1e-6)

    for d in range(1, n):
        coord_copy(d).wait_send()
        value_copy(d).wait_send()
        back_copy(d).wait_send()
        power_copy(d).wait_send()
    for height in range(levels):
        tree_copy(skel_send, skel_recv, s_ss, s_rs, height).wait_send()
        if height < levels - 1:
            tree_copy(lift_send, lift_recv, l_ss, l_rs, height).wait_send()


def fused_local(n, iterate, target, coords, tree_order, leaf_basis, transfer, coupling):
    rhs, width = iterate.shape
    rank = leaf_basis.shape[1]
    share = width // n
    levels = n.bit_length() - 1
    dma = pltpu.SemaphoreType.DMA
    vmem = pltpu.VMEM
    return pl.pallas_call(
        functools.partial(fused, n, levels, EVAL_BLOCKS),
        out_shape=jax.ShapeDtypeStruct((rhs, width), F32),
        in_specs=[pl.BlockSpec(memory_space=vmem)] * 7,
        out_specs=pl.BlockSpec(memory_space=vmem),
        scratch_shapes=[
            vmem((2 * rhs + 16, width), BF16),
            vmem((16, width), F32),
            vmem((width, width), BF16),
            vmem((n, rhs, share), F32),
            vmem((n, 8, share), F32),
            vmem((rhs, width), F32),
            vmem((8, width), F32),
            vmem((16, width), F32),
            vmem((16, width), F32),
            vmem((width, 16), BF16),
            vmem((width, width), BF16),
            vmem((levels, rhs, rank), F32),
            vmem((levels, rhs, rank), F32),
            vmem((levels, rhs, rank), F32),
            vmem((levels, rhs, rank), F32),
            vmem((n, rhs, share), F32),
            vmem((rhs, width), F32),
            vmem((2 * rhs, width), F32),
            vmem((8, 128), F32),
            vmem((n, 8, 128), F32),
            dma((n,)), dma((n,)), dma((n,)), dma((n,)),
            dma((levels,)), dma((levels,)), dma((levels,)), dma((levels,)),
            dma((n,)), dma((n,)), dma((n,)), dma((n,)),
        ],
        compiler_params=pltpu.CompilerParams(
            collective_id=0, has_side_effects=True, vmem_limit_bytes=50 * 2**20
        ),
    )(iterate, target, coords, tree_order, leaf_basis, transfer, coupling)


EVAL_BLOCKS = (4, 5, 6, 8)


def swapped(value, axis, stride):
    mask = 2**stride
    pairs = [(source, source ^ mask) for source in range(lax.axis_size(axis))]
    return lax.ppermute(value, axis, pairs)


def product(left, right):
    return jnp.dot(left, right, precision=lax.Precision.HIGHEST)


def matern_block(left_coords, right_coords):
    squared = (left_coords[0][:, None] - right_coords[0][None, :]) ** 2
    squared = squared + (left_coords[1][:, None] - right_coords[1][None, :]) ** 2
    squared = squared + (left_coords[2][:, None] - right_coords[2][None, :]) ** 2
    scaled = jnp.sqrt(3.0 * squared) * 0.0625
    return (1.0 + scaled) * jnp.exp(-scaled)


def near_field(values, points):
    width = values.shape[1]
    block_rows = min(512, width)

    def accumulate(step_number, running):
        offset = step_number * block_rows
        rows_points = lax.dynamic_slice_in_dim(points, offset, block_rows, 1)
        rows_values = lax.dynamic_slice_in_dim(values, offset, block_rows, 1)
        kernel = matern_block(rows_points, points)
        return running + product(rows_values, kernel)

    summed = lax.fori_loop(0, width // block_rows, accumulate, jnp.zeros(values.shape, jnp.float32))
    return 0.0625 * summed


def pair_step(skeleton, height, tables, couplings, final):
    if final:
        payload = skeleton[None]
    else:
        lifted = product(skeleton, tables[height])
        payload = jnp.stack([skeleton, lifted])
    arrived = swapped(payload, "leaf", height)
    coupled_term = product(arrived[0], couplings[height])
    if final:
        return (coupled_term, skeleton)
    return (coupled_term, lifted + arrived[1])


def local(iterate, target, coords, tree_order, leaf_basis, transfer, coupling):
    devices = lax.axis_size("leaf")
    levels_total = devices.bit_length() - 1
    shuffle = tree_order[0]
    outgoing = (iterate[:, shuffle], coords[:, shuffle].astype(jnp.float32))
    tree_values, tree_coords = (
        lax.all_to_all(outgoing[0], "leaf", split_axis=1, concat_axis=1, tiled=True),
        lax.all_to_all(outgoing[1], "leaf", split_axis=1, concat_axis=1, tiled=True),
    )
    nearby = near_field(tree_values, tree_coords)
    skeleton = jnp.dot(
        tree_values.astype(jnp.bfloat16), leaf_basis, preferred_element_type=jnp.float32
    )
    tables = transfer[0].astype(jnp.float32)
    couplings = coupling[0].astype(jnp.float32)
    coupled = []
    for height in range(levels_total):
        coupled_term, skeleton = pair_step(
            skeleton, height, tables, couplings, height == levels_total - 1
        )
        coupled.append(coupled_term)
    downward = coupled[-1]
    for height in range(levels_total - 2, -1, -1):
        lowered = lax.dot_general(
            downward, tables[height], (((1,), (1,)), ((), ())), precision=lax.Precision.HIGHEST
        )
        downward = coupled[height] + lowered
    far_field = lax.dot_general(
        downward.astype(jnp.bfloat16),
        leaf_basis,
        (((1,), (1,)), ((), ())),
        preferred_element_type=jnp.float32,
    )
    applied = nearby + far_field
    returned = lax.all_to_all(applied, "leaf", split_axis=1, concat_axis=1, tiled=True)
    placed = jnp.zeros_like(target).at[:, shuffle].set(returned)
    residual = target - placed
    power = lax.psum(jnp.sum(residual * residual, axis=1), "leaf")
    return residual / jnp.sqrt(power / (target.shape[1] * devices) + 1e-06)[:, None]


def by_shape(iterate, *rest):
    n = lax.axis_size("leaf")
    rhs, width = iterate.shape
    if n & (n - 1) == 0 and n > 1 and width % (128 * n) == 0 and rhs % 16 == 0 and 128 % rhs == 0:
        return fused_local(n, iterate, *rest)
    return local(iterate, *rest)


def solution(mesh):
    placed = (
        P(("group", "rhs"), "leaf"),
        P(("group", "rhs"), "leaf"),
        P(None, ("group", "leaf")),
        P(("group", "leaf"), None),
        P(("group", "leaf"), None),
        P(("group", "leaf"), None, None, None),
        P(("group", "leaf"), None, None, None),
    )
    return jax.shard_map(
        by_shape, mesh=mesh, in_specs=placed, out_specs=P(("group", "rhs"), "leaf"), check_vma=False
    )
```

```python
import functools
import jax
import jax.numpy as jnp
from jax import lax
from jax.experimental import pallas as pl
from jax.experimental.pallas import tpu as pltpu
from jax.sharding import PartitionSpec as P

F32 = jnp.float32
BF16 = jnp.bfloat16
MESH = pl.DeviceIdType.MESH
ROWS_T = (((1,), (1,)), ((), ()))
COLS_T = (((0,), (0,)), ((), ()))


def far_first(t, n):
    if n == 2:
        return 1 - t
    return n // 2 + ((t + 1) // 2) * (1 - 2 * (t % 2))


def halves(x):
    high = x.astype(BF16)
    low = (x - high.astype(F32)).astype(BF16)
    return jnp.concatenate([high, low], axis=0)


def split_dot(x, right, dims):
    rows = x.shape[0]
    both = lax.dot_general(halves(x), right, dims, preferred_element_type=F32)
    return both[:rows] + both[rows:]


def fused(
    n, levels,
    iterate_h, target_h, coords_h, order_h, basis_h, transfer_h, coupling_h,
    out,
    iterate, target, coords, order, basis, transfer, coupling,
    parts, coord_rows, onehot, send_values, send_coords, tree_values, tree_coords,
    left_feat, right_feat, left_t, kernel_k, skel_send, skel_recv,
    applied, returned, placed, power_send, power_recv,
    in_s, basis_s, c_ss, c_rs, v_ss, v_rs, s_ss, s_rs, b_ss, b_rs, p_ss, p_rs,
):
    rhs, width = iterate.shape
    share = width // n
    me = lax.axis_index("leaf")

    def peer(offset):
        return lax.rem(me + offset, n)

    def source(offset):
        return lax.rem(me + n - offset, n)

    def cols(index):
        return pl.ds(pl.multiple_of(index * share, share), share)

    def slot(index):
        return slice(index * share, (index + 1) * share)

    whole = (order, iterate, coords, transfer, coupling, target)
    loads = [
        pltpu.make_async_copy(src, dst, in_s.at[index]) for index, (src, dst) in enumerate(zip(
            (order_h, iterate_h, coords_h, transfer_h, coupling_h, target_h), whole))]
    for load in loads[:3]:
        load.start()
    basis_loads = [
        pltpu.make_async_copy(basis_h.at[cols(source(d)), :], basis.at[slot(d), :], basis_s.at[d])
        for d in range(n)]

    barrier = pltpu.get_barrier_semaphore()
    for offset in range(1, n):
        pl.semaphore_signal(barrier, inc=1, device_id={"leaf": peer(offset)}, device_id_type=MESH)
    for load in basis_loads + loads[3:]:
        load.start()
    coord_rows[...] = jnp.zeros_like(coord_rows)
    left_feat[...] = jnp.zeros_like(left_feat)
    right_feat[...] = jnp.zeros_like(right_feat)
    for load in loads[:3]:
        load.wait()

    parts[0:2 * rhs, :] = halves(iterate[...])
    coord_rows[0:3, :] = coords[...].astype(F32)
    parts[2 * rhs:2 * rhs + 16, :] = coord_rows[...].astype(BF16)

    def coord_copy(d):
        return pltpu.make_async_remote_copy(
            src_ref=send_coords.at[d], dst_ref=tree_coords.at[:, slot(d)],
            send_sem=c_ss.at[d], recv_sem=c_rs.at[d],
            device_id={"leaf": peer(d)}, device_id_type=MESH)

    def value_copy(d):
        return pltpu.make_async_remote_copy(
            src_ref=send_values.at[d], dst_ref=tree_values.at[:, slot(d)],
            send_sem=v_ss.at[d], recv_sem=v_rs.at[d],
            device_id={"leaf": peer(d)}, device_id_type=MESH)

    for t in range(n):
        d = far_first(t, n)
        spots = lax.broadcasted_iota(jnp.int32, (width, share), 0)
        chosen = (spots == order[:, cols(peer(d))]).astype(F32).astype(BF16)
        onehot[:, slot(d)] = chosen
        moved = jnp.dot(parts[...], chosen, preferred_element_type=F32)
        if d:
            send_values[d] = moved[:rhs] + moved[rhs:2 * rhs]
            send_coords[d] = moved[2 * rhs:2 * rhs + 8]
            if t == 0:
                pl.semaphore_wait(barrier, n - 1)
            coord_copy(d).start()
        else:
            tree_values[:, slot(0)] = moved[:rhs] + moved[rhs:2 * rhs]
            tree_coords[:, slot(0)] = moved[2 * rhs:2 * rhs + 8]
        if t == n - 2:
            for u in range(n - 1):
                value_copy(far_first(u, n)).start()

    for d in range(1, n):
        coord_copy(d).wait_recv()
    xyz = tree_coords[0:3, :]
    norm = jnp.sum(xyz * xyz, axis=0, keepdims=True)
    norm_high = jnp.floor(norm * (1.0 / 256.0))
    norm_low = norm - 256.0 * norm_high
    left_feat[0:3, :] = xyz
    left_feat[3:4, :] = norm_low
    left_feat[4:5, :] = norm_high
    left_feat[5:6, :] = jnp.full_like(norm, 3.0 / 256.0)
    left_feat[6:7, :] = jnp.full_like(norm, 3.0)
    right_feat[0:3, :] = xyz * (-6.0 / 256.0)
    right_feat[3:4, :] = jnp.full_like(norm, 3.0 / 256.0)
    right_feat[4:5, :] = jnp.full_like(norm, 3.0)
    right_feat[5:6, :] = norm_low
    right_feat[6:7, :] = norm_high
    left_t[...] = left_feat[...].T.astype(BF16)

    def matern_column(j):
        right = right_feat[:, slot(j)].astype(BF16)
        for i in range(j + 1):
            q = jnp.dot(left_t[slot(i), :], right, preferred_element_type=F32)
            s = q * lax.rsqrt(jnp.maximum(q, 1e-30))
            kernel_k[slot(i), slot(j)] = ((1.0 + s) * jnp.exp2(s * (-1.4426950408889634))).astype(BF16)

    early = (5 * n) // 8
    for j in range(early):
        matern_column(j)

    for load in basis_loads + loads[3:]:
        load.wait()
    for d in range(1, n):
        value_copy(d).wait_recv()
    plain = (((1,), (0,)), ((), ()))
    skeleton = [jnp.dot(tree_values[...].astype(BF16), basis[...], preferred_element_type=F32)]
    for height in range(levels - 1):
        skeleton.append(split_dot(skeleton[height], transfer[0, height], plain))
    for height in range(levels):
        skel_send[height] = skeleton[height]

    def tree_copy(height, turn):
        size = 2 ** height
        node = me // size
        sibling = node + 1 - 2 * lax.rem(node, 2)
        index = size - 1 + turn
        return pltpu.make_async_remote_copy(
            src_ref=skel_send.at[height], dst_ref=skel_recv.at[index],
            send_sem=s_ss.at[index], recv_sem=s_rs.at[index],
            device_id={"leaf": sibling * size + lax.rem(me + turn, size)}, device_id_type=MESH)

    tree_copies = [tree_copy(height, turn) for height in reversed(range(levels)) for turn in range(2 ** height)]
    for copy in tree_copies:
        copy.start()

    for j in range(early, n):
        matern_column(j)
    values = halves(tree_values[...])
    for j in range(n):
        cut = (j + 1) * share
        near = jnp.dot(values[:, :cut], kernel_k[:cut, slot(j)], preferred_element_type=F32)
        if j < n - 1:
            near += lax.dot_general(values[:, cut:], kernel_k[slot(j), cut:], ROWS_T,
                                    preferred_element_type=F32)
        applied[j] = 0.0625 * (near[:rhs] + near[rhs:])

    for copy in tree_copies:
        copy.wait_recv()
    coupled = []
    for height in range(levels):
        first = 2 ** height - 1
        gathered = skel_recv[first]
        for turn in range(1, 2 ** height):
            gathered = gathered + skel_recv[first + turn]
        coupled.append(split_dot(gathered, coupling[0, height], plain))
    downward = coupled[-1]
    for height in range(levels - 2, -1, -1):
        downward = coupled[height] + split_dot(downward, transfer[0, height], ROWS_T)
    down = downward.astype(BF16)

    def back_copy(d):
        return pltpu.make_async_remote_copy(
            src_ref=applied.at[d], dst_ref=returned.at[:, slot(d)],
            send_sem=b_ss.at[d], recv_sem=b_rs.at[d],
            device_id={"leaf": source(d)}, device_id_type=MESH)

    for t in range(n):
        d = far_first(t, n)
        far = lax.dot_general(down, basis[slot(d), :], ROWS_T, preferred_element_type=F32)
        if d:
            applied[d] += far
            back_copy(d).start()
        else:
            returned[:, slot(0)] = applied[0] + far

    def put_back(d):
        return lax.dot_general(halves(returned[:, slot(d)]), onehot[:, slot(d)], ROWS_T,
                               preferred_element_type=F32)

    placed[...] = put_back(0)
    for t in range(n - 2, -1, -1):
        d = far_first(t, n)
        back_copy(d).wait_recv()
        placed[...] += put_back(d)
    residual = target[...] - (placed[:rhs] + placed[rhs:])
    power = jnp.sum(residual * residual, axis=1, keepdims=True)

    tall = jnp.broadcast_to(power, (rhs, 128))
    square = jnp.concatenate([tall] * (128 // rhs), axis=0)
    power_send[...] = square.T[0:8, :]

    def power_copy(d):
        return pltpu.make_async_remote_copy(
            src_ref=power_send, dst_ref=power_recv.at[d],
            send_sem=p_ss.at[d], recv_sem=p_rs.at[d],
            device_id={"leaf": peer(d)}, device_id_type=MESH)

    for t in range(n - 1):
        power_copy(far_first(t, n)).start()
    summed = power_send[...]
    for d in range(1, n):
        power_copy(d).wait_recv()
        summed = summed + power_recv[d]
    total_power = jnp.concatenate([summed] * 16, axis=0).T[0:rhs, 0:1]
    out[...] = residual * lax.rsqrt(total_power * (1.0 / (width * n)) + 1e-6)

    for d in range(1, n):
        coord_copy(d).wait_send()
        value_copy(d).wait_send()
        back_copy(d).wait_send()
        power_copy(d).wait_send()
    for copy in tree_copies:
        copy.wait_send()


def fused_local(n, iterate, target, coords, tree_order, leaf_basis, transfer, coupling):
    rhs, width = iterate.shape
    rank = leaf_basis.shape[1]
    share = width // n
    levels = n.bit_length() - 1
    dma = pltpu.SemaphoreType.DMA
    vmem = pltpu.VMEM
    return pl.pallas_call(
        functools.partial(fused, n, levels),
        out_shape=jax.ShapeDtypeStruct((rhs, width), F32),
        in_specs=[pl.BlockSpec(memory_space=pltpu.HBM)] * 7,
        out_specs=pl.BlockSpec(memory_space=vmem),
        scratch_shapes=[
            vmem(iterate.shape, F32),
            vmem(target.shape, F32),
            vmem(coords.shape, jnp.int32),
            vmem(tree_order.shape, jnp.int32),
            vmem(leaf_basis.shape, BF16),
            vmem(transfer.shape, BF16),
            vmem(coupling.shape, BF16),
            vmem((2 * rhs + 16, width), BF16),
            vmem((16, width), F32),
            vmem((width, width), BF16),
            vmem((n, rhs, share), F32),
            vmem((n, 8, share), F32),
            vmem((rhs, width), F32),
            vmem((8, width), F32),
            vmem((16, width), F32),
            vmem((16, width), F32),
            vmem((width, 16), BF16),
            vmem((width, width), BF16),
            vmem((levels, rhs, rank), F32),
            vmem((n, rhs, rank), F32),
            vmem((n, rhs, share), F32),
            vmem((rhs, width), F32),
            vmem((2 * rhs, width), F32),
            vmem((8, 128), F32),
            vmem((n, 8, 128), F32),
            dma((6,)), dma((n,)),
            dma((n,)), dma((n,)), dma((n,)), dma((n,)),
            dma((n,)), dma((n,)), dma((n,)), dma((n,)), dma((n,)), dma((n,)),
        ],
        compiler_params=pltpu.CompilerParams(
            collective_id=0, has_side_effects=True, vmem_limit_bytes=50 * 2**20
        ),
    )(iterate, target, coords, tree_order, leaf_basis, transfer, coupling)


def swapped(value, axis, stride):
    mask = 2**stride
    pairs = [(source, source ^ mask) for source in range(lax.axis_size(axis))]
    return lax.ppermute(value, axis, pairs)


def product(left, right):
    return jnp.dot(left, right, precision=lax.Precision.HIGHEST)


def matern_block(left_coords, right_coords):
    squared = (left_coords[0][:, None] - right_coords[0][None, :]) ** 2
    squared = squared + (left_coords[1][:, None] - right_coords[1][None, :]) ** 2
    squared = squared + (left_coords[2][:, None] - right_coords[2][None, :]) ** 2
    scaled = jnp.sqrt(3.0 * squared) * 0.0625
    return (1.0 + scaled) * jnp.exp(-scaled)


def near_field(values, points):
    width = values.shape[1]
    block_rows = min(512, width)

    def accumulate(step_number, running):
        offset = step_number * block_rows
        rows_points = lax.dynamic_slice_in_dim(points, offset, block_rows, 1)
        rows_values = lax.dynamic_slice_in_dim(values, offset, block_rows, 1)
        kernel = matern_block(rows_points, points)
        return running + product(rows_values, kernel)

    summed = lax.fori_loop(0, width // block_rows, accumulate, jnp.zeros(values.shape, jnp.float32))
    return 0.0625 * summed


def pair_step(skeleton, height, tables, couplings, final):
    if final:
        payload = skeleton[None]
    else:
        lifted = product(skeleton, tables[height])
        payload = jnp.stack([skeleton, lifted])
    arrived = swapped(payload, "leaf", height)
    coupled_term = product(arrived[0], couplings[height])
    if final:
        return (coupled_term, skeleton)
    return (coupled_term, lifted + arrived[1])


def local(iterate, target, coords, tree_order, leaf_basis, transfer, coupling):
    devices = lax.axis_size("leaf")
    levels_total = devices.bit_length() - 1
    shuffle = tree_order[0]
    outgoing = (iterate[:, shuffle], coords[:, shuffle].astype(jnp.float32))
    tree_values, tree_coords = (
        lax.all_to_all(outgoing[0], "leaf", split_axis=1, concat_axis=1, tiled=True),
        lax.all_to_all(outgoing[1], "leaf", split_axis=1, concat_axis=1, tiled=True),
    )
    nearby = near_field(tree_values, tree_coords)
    skeleton = jnp.dot(
        tree_values.astype(jnp.bfloat16), leaf_basis, preferred_element_type=jnp.float32
    )
    tables = transfer[0].astype(jnp.float32)
    couplings = coupling[0].astype(jnp.float32)
    coupled = []
    for height in range(levels_total):
        coupled_term, skeleton = pair_step(
            skeleton, height, tables, couplings, height == levels_total - 1
        )
        coupled.append(coupled_term)
    downward = coupled[-1]
    for height in range(levels_total - 2, -1, -1):
        lowered = lax.dot_general(
            downward, tables[height], (((1,), (1,)), ((), ())), precision=lax.Precision.HIGHEST
        )
        downward = coupled[height] + lowered
    far_field = lax.dot_general(
        downward.astype(jnp.bfloat16),
        leaf_basis,
        (((1,), (1,)), ((), ())),
        preferred_element_type=jnp.float32,
    )
    applied = nearby + far_field
    returned = lax.all_to_all(applied, "leaf", split_axis=1, concat_axis=1, tiled=True)
    placed = jnp.zeros_like(target).at[:, shuffle].set(returned)
    residual = target - placed
    power = lax.psum(jnp.sum(residual * residual, axis=1), "leaf")
    return residual / jnp.sqrt(power / (target.shape[1] * devices) + 1e-06)[:, None]


def by_shape(iterate, *rest):
    n = lax.axis_size("leaf")
    rhs, width = iterate.shape
    if n & (n - 1) == 0 and n > 1 and width % (128 * n) == 0 and rhs % 16 == 0 and 128 % rhs == 0:
        return fused_local(n, iterate, *rest)
    return local(iterate, *rest)


def solution(mesh):
    placed = (
        P(("group", "rhs"), "leaf"),
        P(("group", "rhs"), "leaf"),
        P(None, ("group", "leaf")),
        P(("group", "leaf"), None),
        P(("group", "leaf"), None),
        P(("group", "leaf"), None, None, None),
        P(("group", "leaf"), None, None, None),
    )
    return jax.shard_map(
        by_shape, mesh=mesh, in_specs=placed, out_specs=P(("group", "rhs"), "leaf"), check_vma=False
    )
```

```python
import functools
import jax
import jax.numpy as jnp
from jax import lax
from jax.experimental import pallas as pl
from jax.experimental.pallas import tpu as pltpu
from jax.sharding import PartitionSpec as P

F32 = jnp.float32
BF16 = jnp.bfloat16
MESH = pl.DeviceIdType.MESH
ROWS_T = (((1,), (1,)), ((), ()))
COLS_T = (((0,), (0,)), ((), ()))


def far_first(t, n):
    if n == 2:
        return 1 - t
    return n // 2 + ((t + 1) // 2) * (1 - 2 * (t % 2))


def halves(x):
    high = x.astype(BF16)
    low = (x - high.astype(F32)).astype(BF16)
    return jnp.concatenate([high, low], axis=0)


def split_dot(x, right, dims):
    rows = x.shape[0]
    both = lax.dot_general(halves(x), right, dims, preferred_element_type=F32)
    return both[:rows] + both[rows:]


def fused(
    n, levels,
    iterate_h, target_h, coords_h, order_h, basis_h, transfer_h, coupling_h,
    out,
    iterate, target, coords, order, basis, transfer, coupling,
    parts, coord_rows, onehot, send_values, send_coords, tree_values, tree_coords,
    left_feat, right_feat, left_t, kernel_k, skel_send, skel_recv,
    applied, returned, placed, power_send, power_recv,
    in_s, basis_s, c_ss, c_rs, v_ss, v_rs, s_ss, s_rs, b_ss, b_rs, p_ss, p_rs,
):
    rhs, width = iterate.shape
    share = width // n
    me = lax.axis_index("leaf")

    def peer(offset):
        return lax.rem(me + offset, n)

    def source(offset):
        return lax.rem(me + n - offset, n)

    def cols(index):
        return pl.ds(pl.multiple_of(index * share, share), share)

    def slot(index):
        return slice(index * share, (index + 1) * share)

    whole = (order, iterate, coords, transfer, coupling, target)
    loads = [
        pltpu.make_async_copy(src, dst, in_s.at[index]) for index, (src, dst) in enumerate(zip(
            (order_h, iterate_h, coords_h, transfer_h, coupling_h, target_h), whole))]
    for load in loads[:3]:
        load.start()
    basis_loads = [
        pltpu.make_async_copy(basis_h.at[cols(source(d)), :], basis.at[slot(d), :], basis_s.at[d])
        for d in range(n)]

    barrier = pltpu.get_barrier_semaphore()
    for offset in range(1, n):
        pl.semaphore_signal(barrier, inc=1, device_id={"leaf": peer(offset)}, device_id_type=MESH)
    for load in basis_loads + loads[3:]:
        load.start()
    coord_rows[...] = jnp.zeros_like(coord_rows)
    left_feat[...] = jnp.zeros_like(left_feat)
    right_feat[...] = jnp.zeros_like(right_feat)
    for load in loads[:3]:
        load.wait()

    parts[0:2 * rhs, :] = halves(iterate[...])
    coord_rows[0:3, :] = coords[...].astype(F32)
    parts[2 * rhs:2 * rhs + 16, :] = coord_rows[...].astype(BF16)

    def coord_copy(d):
        return pltpu.make_async_remote_copy(
            src_ref=send_coords.at[d], dst_ref=tree_coords.at[:, slot(d)],
            send_sem=c_ss.at[d], recv_sem=c_rs.at[d],
            device_id={"leaf": peer(d)}, device_id_type=MESH)

    def value_copy(d):
        return pltpu.make_async_remote_copy(
            src_ref=send_values.at[d], dst_ref=tree_values.at[:, slot(d)],
            send_sem=v_ss.at[d], recv_sem=v_rs.at[d],
            device_id={"leaf": peer(d)}, device_id_type=MESH)

    for t in range(n):
        d = far_first(t, n)
        spots = lax.broadcasted_iota(jnp.int32, (width, share), 0)
        chosen = (spots == order[:, cols(peer(d))]).astype(F32).astype(BF16)
        onehot[:, slot(d)] = chosen
        moved = jnp.dot(parts[...], chosen, preferred_element_type=F32)
        if d:
            send_values[d] = moved[:rhs] + moved[rhs:2 * rhs]
            send_coords[d] = moved[2 * rhs:2 * rhs + 8]
            if t == 0:
                pl.semaphore_wait(barrier, n - 1)
            coord_copy(d).start()
        else:
            tree_values[:, slot(0)] = moved[:rhs] + moved[rhs:2 * rhs]
            tree_coords[:, slot(0)] = moved[2 * rhs:2 * rhs + 8]
        if t == n - 2:
            for u in range(n - 1):
                value_copy(far_first(u, n)).start()

    for d in range(1, n):
        coord_copy(d).wait_recv()
    xyz = tree_coords[0:3, :]
    norm = jnp.sum(xyz * xyz, axis=0, keepdims=True)
    norm_high = jnp.floor(norm * (1.0 / 256.0))
    norm_low = norm - 256.0 * norm_high
    left_feat[0:3, :] = xyz
    left_feat[3:4, :] = norm_low
    left_feat[4:5, :] = norm_high
    left_feat[5:6, :] = jnp.full_like(norm, 3.0 / 256.0)
    left_feat[6:7, :] = jnp.full_like(norm, 3.0)
    right_feat[0:3, :] = xyz * (-6.0 / 256.0)
    right_feat[3:4, :] = jnp.full_like(norm, 3.0 / 256.0)
    right_feat[4:5, :] = jnp.full_like(norm, 3.0)
    right_feat[5:6, :] = norm_low
    right_feat[6:7, :] = norm_high
    left_t[...] = left_feat[...].T.astype(BF16)

    def matern_column(j):
        right = right_feat[:, slot(j)].astype(BF16)
        for i in range(j + 1):
            q = jnp.dot(left_t[slot(i), :], right, preferred_element_type=F32)
            s = q * lax.rsqrt(jnp.maximum(q, 1e-30))
            kernel_k[slot(i), slot(j)] = ((1.0 + s) * jnp.exp2(s * (-1.4426950408889634))).astype(BF16)

    early = (5 * n) // 8
    for j in range(early):
        matern_column(j)

    for load in basis_loads + loads[3:]:
        load.wait()
    for d in range(1, n):
        value_copy(d).wait_recv()
    plain = (((1,), (0,)), ((), ()))
    skeleton = [jnp.dot(tree_values[...].astype(BF16), basis[...], preferred_element_type=F32)]
    for height in range(levels - 1):
        skeleton.append(split_dot(skeleton[height], transfer[0, height], plain))
    for height in range(levels):
        skel_send[height] = skeleton[height]

    def tree_copy(height, turn):
        size = 2 ** height
        node = me // size
        sibling = node + 1 - 2 * lax.rem(node, 2)
        index = size - 1 + turn
        return pltpu.make_async_remote_copy(
            src_ref=skel_send.at[height], dst_ref=skel_recv.at[index],
            send_sem=s_ss.at[index], recv_sem=s_rs.at[index],
            device_id={"leaf": sibling * size + lax.rem(me + turn, size)}, device_id_type=MESH)

    tree_copies = [tree_copy(height, turn) for height in reversed(range(levels)) for turn in range(2 ** height)]
    for copy in tree_copies:
        copy.start()

    for j in range(early, n):
        matern_column(j)
    values = halves(tree_values[...])
    for j in range(n):
        cut = (j + 1) * share
        near = jnp.dot(values[:, :cut], kernel_k[:cut, slot(j)], preferred_element_type=F32)
        if j < n - 1:
            near += lax.dot_general(values[:, cut:], kernel_k[slot(j), cut:], ROWS_T,
                                    preferred_element_type=F32)
        applied[j] = 0.0625 * (near[:rhs] + near[rhs:])

    for copy in tree_copies:
        copy.wait_recv()
    coupled = []
    for height in range(levels):
        first = 2 ** height - 1
        gathered = skel_recv[first]
        for turn in range(1, 2 ** height):
            gathered = gathered + skel_recv[first + turn]
        coupled.append(split_dot(gathered, coupling[0, height], plain))
    downward = coupled[-1]
    for height in range(levels - 2, -1, -1):
        downward = coupled[height] + split_dot(downward, transfer[0, height], ROWS_T)
    down = downward.astype(BF16)

    def back_copy(d):
        return pltpu.make_async_remote_copy(
            src_ref=applied.at[d], dst_ref=returned.at[:, slot(d)],
            send_sem=b_ss.at[d], recv_sem=b_rs.at[d],
            device_id={"leaf": source(d)}, device_id_type=MESH)

    for t in range(n):
        d = far_first(t, n)
        far = lax.dot_general(down, basis[slot(d), :], ROWS_T, preferred_element_type=F32)
        if d:
            applied[d] += far
            back_copy(d).start()
        else:
            returned[:, slot(0)] = applied[0] + far

    def put_back(d):
        return lax.dot_general(halves(returned[:, slot(d)]), onehot[:, slot(d)], ROWS_T,
                               preferred_element_type=F32)

    placed[...] = put_back(0)
    for t in range(n - 2, -1, -1):
        d = far_first(t, n)
        back_copy(d).wait_recv()
        placed[...] += put_back(d)
    residual = target[...] - (placed[:rhs] + placed[rhs:])
    power = jnp.sum(residual * residual, axis=1, keepdims=True)

    tall = jnp.broadcast_to(power, (rhs, 128))
    square = jnp.concatenate([tall] * (128 // rhs), axis=0)
    power_send[...] = square.T[0:8, :]

    def power_copy(d):
        return pltpu.make_async_remote_copy(
            src_ref=power_send, dst_ref=power_recv.at[d],
            send_sem=p_ss.at[d], recv_sem=p_rs.at[d],
            device_id={"leaf": peer(d)}, device_id_type=MESH)

    for t in range(n - 1):
        power_copy(far_first(t, n)).start()
    summed = power_send[...]
    for d in range(1, n):
        power_copy(d).wait_recv()
        summed = summed + power_recv[d]
    total_power = jnp.concatenate([summed] * 16, axis=0).T[0:rhs, 0:1]
    out[...] = residual * lax.rsqrt(total_power * (1.0 / (width * n)) + 1e-6)

    for d in range(1, n):
        coord_copy(d).wait_send()
        value_copy(d).wait_send()
        back_copy(d).wait_send()
        power_copy(d).wait_send()
    for copy in tree_copies:
        copy.wait_send()


def fused_local(n, iterate, target, coords, tree_order, leaf_basis, transfer, coupling):
    rhs, width = iterate.shape
    rank = leaf_basis.shape[1]
    share = width // n
    levels = n.bit_length() - 1
    dma = pltpu.SemaphoreType.DMA
    vmem = pltpu.VMEM
    return pl.pallas_call(
        functools.partial(fused, n, levels),
        out_shape=jax.ShapeDtypeStruct((rhs, width), F32),
        in_specs=[pl.BlockSpec(memory_space=pltpu.HBM)] * 7,
        out_specs=pl.BlockSpec(memory_space=vmem),
        scratch_shapes=[
            vmem(iterate.shape, F32),
            vmem(target.shape, F32),
            vmem(coords.shape, jnp.int32),
            vmem(tree_order.shape, jnp.int32),
            vmem(leaf_basis.shape, BF16),
            vmem(transfer.shape, BF16),
            vmem(coupling.shape, BF16),
            vmem((2 * rhs + 16, width), BF16),
            vmem((16, width), F32),
            vmem((width, width), BF16),
            vmem((n, rhs, share), F32),
            vmem((n, 8, share), F32),
            vmem((rhs, width), F32),
            vmem((8, width), F32),
            vmem((16, width), F32),
            vmem((16, width), F32),
            vmem((width, 16), BF16),
            vmem((width, width), BF16),
            vmem((levels, rhs, rank), F32),
            vmem((n, rhs, rank), F32),
            vmem((n, rhs, share), F32),
            vmem((rhs, width), F32),
            vmem((2 * rhs, width), F32),
            vmem((8, 128), F32),
            vmem((n, 8, 128), F32),
            dma((6,)), dma((n,)),
            dma((n,)), dma((n,)), dma((n,)), dma((n,)),
            dma((n,)), dma((n,)), dma((n,)), dma((n,)), dma((n,)), dma((n,)),
        ],
        compiler_params=pltpu.CompilerParams(
            collective_id=0, has_side_effects=True, vmem_limit_bytes=60 * 2**20
        ),
    )(iterate, target, coords, tree_order, leaf_basis, transfer, coupling)


def swapped(value, axis, stride):
    mask = 2**stride
    pairs = [(source, source ^ mask) for source in range(lax.axis_size(axis))]
    return lax.ppermute(value, axis, pairs)


def product(left, right):
    return jnp.dot(left, right, precision=lax.Precision.HIGHEST)


def matern_block(left_coords, right_coords):
    squared = (left_coords[0][:, None] - right_coords[0][None, :]) ** 2
    squared = squared + (left_coords[1][:, None] - right_coords[1][None, :]) ** 2
    squared = squared + (left_coords[2][:, None] - right_coords[2][None, :]) ** 2
    scaled = jnp.sqrt(3.0 * squared) * 0.0625
    return (1.0 + scaled) * jnp.exp(-scaled)


def near_field(values, points):
    width = values.shape[1]
    block_rows = min(512, width)

    def accumulate(step_number, running):
        offset = step_number * block_rows
        rows_points = lax.dynamic_slice_in_dim(points, offset, block_rows, 1)
        rows_values = lax.dynamic_slice_in_dim(values, offset, block_rows, 1)
        kernel = matern_block(rows_points, points)
        return running + product(rows_values, kernel)

    summed = lax.fori_loop(0, width // block_rows, accumulate, jnp.zeros(values.shape, jnp.float32))
    return 0.0625 * summed


def pair_step(skeleton, height, tables, couplings, final):
    if final:
        payload = skeleton[None]
    else:
        lifted = product(skeleton, tables[height])
        payload = jnp.stack([skeleton, lifted])
    arrived = swapped(payload, "leaf", height)
    coupled_term = product(arrived[0], couplings[height])
    if final:
        return (coupled_term, skeleton)
    return (coupled_term, lifted + arrived[1])


def local(iterate, target, coords, tree_order, leaf_basis, transfer, coupling):
    devices = lax.axis_size("leaf")
    levels_total = devices.bit_length() - 1
    shuffle = tree_order[0]
    outgoing = (iterate[:, shuffle], coords[:, shuffle].astype(jnp.float32))
    tree_values, tree_coords = (
        lax.all_to_all(outgoing[0], "leaf", split_axis=1, concat_axis=1, tiled=True),
        lax.all_to_all(outgoing[1], "leaf", split_axis=1, concat_axis=1, tiled=True),
    )
    nearby = near_field(tree_values, tree_coords)
    skeleton = jnp.dot(
        tree_values.astype(jnp.bfloat16), leaf_basis, preferred_element_type=jnp.float32
    )
    tables = transfer[0].astype(jnp.float32)
    couplings = coupling[0].astype(jnp.float32)
    coupled = []
    for height in range(levels_total):
        coupled_term, skeleton = pair_step(
            skeleton, height, tables, couplings, height == levels_total - 1
        )
        coupled.append(coupled_term)
    downward = coupled[-1]
    for height in range(levels_total - 2, -1, -1):
        lowered = lax.dot_general(
            downward, tables[height], (((1,), (1,)), ((), ())), precision=lax.Precision.HIGHEST
        )
        downward = coupled[height] + lowered
    far_field = lax.dot_general(
        downward.astype(jnp.bfloat16),
        leaf_basis,
        (((1,), (1,)), ((), ())),
        preferred_element_type=jnp.float32,
    )
    applied = nearby + far_field
    returned = lax.all_to_all(applied, "leaf", split_axis=1, concat_axis=1, tiled=True)
    placed = jnp.zeros_like(target).at[:, shuffle].set(returned)
    residual = target - placed
    power = lax.psum(jnp.sum(residual * residual, axis=1), "leaf")
    return residual / jnp.sqrt(power / (target.shape[1] * devices) + 1e-06)[:, None]


def by_shape(iterate, *rest):
    n = lax.axis_size("leaf")
    rhs, width = iterate.shape
    if n & (n - 1) == 0 and n > 1 and width % (128 * n) == 0 and rhs % 16 == 0 and 128 % rhs == 0:
        return fused_local(n, iterate, *rest)
    return local(iterate, *rest)


def solution(mesh):
    placed = (
        P(("group", "rhs"), "leaf"),
        P(("group", "rhs"), "leaf"),
        P(None, ("group", "leaf")),
        P(("group", "leaf"), None),
        P(("group", "leaf"), None),
        P(("group", "leaf"), None, None, None),
        P(("group", "leaf"), None, None, None),
    )
    return jax.shard_map(
        by_shape, mesh=mesh, in_specs=placed, out_specs=P(("group", "rhs"), "leaf"), check_vma=False
    )
```

```python
import functools
import jax
import jax.numpy as jnp
from jax import lax
from jax.experimental import pallas as pl
from jax.experimental.pallas import tpu as pltpu
from jax.sharding import PartitionSpec as P

F32 = jnp.float32
BF16 = jnp.bfloat16
MESH = pl.DeviceIdType.MESH
ROWS_T = (((1,), (1,)), ((), ()))
COLS_T = (((0,), (0,)), ((), ()))


def far_first(t, n):
    if n == 2:
        return 1 - t
    return n // 2 + ((t + 1) // 2) * (1 - 2 * (t % 2))


def halves(x):
    high = x.astype(BF16)
    low = (x - high.astype(F32)).astype(BF16)
    return jnp.concatenate([high, low], axis=0)


def split_dot(x, right, dims):
    rows = x.shape[0]
    both = lax.dot_general(halves(x), right, dims, preferred_element_type=F32)
    return both[:rows] + both[rows:]


def fused(
    n, levels,
    iterate_h, target_h, coords_h, order_h, basis_h, transfer_h, coupling_h,
    out,
    iterate, target, coords, order, basis, transfer, coupling,
    parts, coord_rows, onehot, send_values, send_coords, tree_values, tree_coords,
    left_feat, right_feat, left_t, kernel_k, skel_send, skel_recv,
    applied, returned, placed, power_send, power_recv,
    in_s, basis_s, c_ss, c_rs, v_ss, v_rs, s_ss, s_rs, b_ss, b_rs, p_ss, p_rs,
):
    rhs, width = iterate.shape
    share = width // n
    me = lax.axis_index("leaf")

    def peer(offset):
        return lax.rem(me + offset, n)

    def source(offset):
        return lax.rem(me + n - offset, n)

    def cols(index):
        return pl.ds(pl.multiple_of(index * share, share), share)

    def slot(index):
        return slice(index * share, (index + 1) * share)

    whole = (order, iterate, coords, transfer, coupling, target)
    loads = [
        pltpu.make_async_copy(src, dst, in_s.at[index]) for index, (src, dst) in enumerate(zip(
            (order_h, iterate_h, coords_h, transfer_h, coupling_h, target_h), whole))]
    for load in loads[:3]:
        load.start()
    basis_loads = [
        pltpu.make_async_copy(basis_h.at[cols(source(d)), :], basis.at[slot(d), :], basis_s.at[d])
        for d in range(n)]

    barrier = pltpu.get_barrier_semaphore()
    for offset in range(1, n):
        pl.semaphore_signal(barrier, inc=1, device_id={"leaf": peer(offset)}, device_id_type=MESH)
    for load in basis_loads + loads[3:]:
        load.start()
    coord_rows[...] = jnp.zeros_like(coord_rows)
    left_feat[...] = jnp.zeros_like(left_feat)
    right_feat[...] = jnp.zeros_like(right_feat)
    for load in loads[:3]:
        load.wait()

    parts[0:2 * rhs, :] = halves(iterate[...])
    coord_rows[0:3, :] = coords[...].astype(F32)
    parts[2 * rhs:2 * rhs + 16, :] = coord_rows[...].astype(BF16)

    def coord_copy(d):
        return pltpu.make_async_remote_copy(
            src_ref=send_coords.at[d], dst_ref=tree_coords.at[:, slot(d)],
            send_sem=c_ss.at[d], recv_sem=c_rs.at[d],
            device_id={"leaf": peer(d)}, device_id_type=MESH)

    def value_copy(d):
        return pltpu.make_async_remote_copy(
            src_ref=send_values.at[d], dst_ref=tree_values.at[:, slot(d)],
            send_sem=v_ss.at[d], recv_sem=v_rs.at[d],
            device_id={"leaf": peer(d)}, device_id_type=MESH)

    for t in range(n):
        d = far_first(t, n)
        spots = lax.broadcasted_iota(jnp.int32, (width, share), 0).astype(jnp.int16)
        wanted = jnp.broadcast_to(order[:, cols(peer(d))], (16, share)).astype(jnp.int16)
        wanted = jnp.concatenate([wanted] * (width // 16), axis=0)
        chosen = jnp.where(spots == wanted, jnp.ones((), BF16), jnp.zeros((), BF16))
        onehot[:, slot(d)] = chosen
        moved = jnp.dot(parts[...], chosen, preferred_element_type=F32)
        if d:
            send_values[d] = moved[:rhs] + moved[rhs:2 * rhs]
            send_coords[d] = moved[2 * rhs:2 * rhs + 8]
            if t == 0:
                pl.semaphore_wait(barrier, n - 1)
            coord_copy(d).start()
        else:
            tree_values[:, slot(0)] = moved[:rhs] + moved[rhs:2 * rhs]
            tree_coords[:, slot(0)] = moved[2 * rhs:2 * rhs + 8]
        if t == n - 2:
            for u in range(n - 1):
                value_copy(far_first(u, n)).start()

    for d in range(1, n):
        coord_copy(d).wait_recv()
    xyz = tree_coords[0:3, :]
    norm = jnp.sum(xyz * xyz, axis=0, keepdims=True)
    norm_high = jnp.floor(norm * (1.0 / 256.0))
    norm_low = norm - 256.0 * norm_high
    left_feat[0:3, :] = xyz
    left_feat[3:4, :] = norm_low
    left_feat[4:5, :] = norm_high
    left_feat[5:6, :] = jnp.full_like(norm, 3.0 / 256.0)
    left_feat[6:7, :] = jnp.full_like(norm, 3.0)
    right_feat[0:3, :] = xyz * (-6.0 / 256.0)
    right_feat[3:4, :] = jnp.full_like(norm, 3.0 / 256.0)
    right_feat[4:5, :] = jnp.full_like(norm, 3.0)
    right_feat[5:6, :] = norm_low
    right_feat[6:7, :] = norm_high
    left_t[...] = left_feat[...].T.astype(BF16)

    def matern_column(j):
        right = right_feat[:, slot(j)].astype(BF16)
        for i in range(j + 1):
            q = jnp.dot(left_t[slot(i), :], right, preferred_element_type=F32)
            s = q * lax.rsqrt(jnp.maximum(q, 1e-30))
            kernel_k[slot(i), slot(j)] = ((1.0 + s) * jnp.exp2(s * (-1.4426950408889634))).astype(BF16)

    early = n
    for j in range(early):
        matern_column(j)

    for load in basis_loads + loads[3:]:
        load.wait()
    for d in range(1, n):
        value_copy(d).wait_recv()
    plain = (((1,), (0,)), ((), ()))
    skeleton = [jnp.dot(tree_values[...].astype(BF16), basis[...], preferred_element_type=F32)]
    for height in range(levels - 1):
        skeleton.append(split_dot(skeleton[height], transfer[0, height], plain))
    for height in range(levels):
        skel_send[height] = skeleton[height]

    def tree_copy(height, turn):
        size = 2 ** height
        node = me // size
        sibling = node + 1 - 2 * lax.rem(node, 2)
        index = size - 1 + turn
        return pltpu.make_async_remote_copy(
            src_ref=skel_send.at[height], dst_ref=skel_recv.at[index],
            send_sem=s_ss.at[index], recv_sem=s_rs.at[index],
            device_id={"leaf": sibling * size + lax.rem(me + turn, size)}, device_id_type=MESH)

    tree_copies = [tree_copy(height, turn) for height in reversed(range(levels)) for turn in range(2 ** height)]
    for copy in tree_copies:
        copy.start()

    for j in range(early, n):
        matern_column(j)
    values = halves(tree_values[...])
    for j in range(n):
        cut = (j + 1) * share
        near = jnp.dot(values[:, :cut], kernel_k[:cut, slot(j)], preferred_element_type=F32)
        if j < n - 1:
            near += lax.dot_general(values[:, cut:], kernel_k[slot(j), cut:], ROWS_T,
                                    preferred_element_type=F32)
        applied[j] = 0.0625 * (near[:rhs] + near[rhs:])

    for copy in tree_copies:
        copy.wait_recv()
    coupled = []
    for height in range(levels):
        first = 2 ** height - 1
        gathered = skel_recv[first]
        for turn in range(1, 2 ** height):
            gathered = gathered + skel_recv[first + turn]
        coupled.append(split_dot(gathered, coupling[0, height], plain))
    downward = coupled[-1]
    for height in range(levels - 2, -1, -1):
        downward = coupled[height] + split_dot(downward, transfer[0, height], ROWS_T)
    down = downward.astype(BF16)

    def back_copy(d):
        return pltpu.make_async_remote_copy(
            src_ref=applied.at[d], dst_ref=returned.at[:, slot(d)],
            send_sem=b_ss.at[d], recv_sem=b_rs.at[d],
            device_id={"leaf": source(d)}, device_id_type=MESH)

    for t in range(n):
        d = far_first(t, n)
        far = lax.dot_general(down, basis[slot(d), :], ROWS_T, preferred_element_type=F32)
        if d:
            applied[d] += far
            back_copy(d).start()
        else:
            returned[:, slot(0)] = applied[0] + far

    def put_back(d):
        return lax.dot_general(halves(returned[:, slot(d)]), onehot[:, slot(d)], ROWS_T,
                               preferred_element_type=F32)

    placed[...] = put_back(0)
    for t in range(n - 2, -1, -1):
        d = far_first(t, n)
        back_copy(d).wait_recv()
        placed[...] += put_back(d)
    residual = target[...] - (placed[:rhs] + placed[rhs:])
    power = jnp.sum(residual * residual, axis=1, keepdims=True)

    tall = jnp.broadcast_to(power, (rhs, 128))
    square = jnp.concatenate([tall] * (128 // rhs), axis=0)
    power_send[...] = square.T[0:8, :]

    def power_copy(d):
        return pltpu.make_async_remote_copy(
            src_ref=power_send, dst_ref=power_recv.at[d],
            send_sem=p_ss.at[d], recv_sem=p_rs.at[d],
            device_id={"leaf": peer(d)}, device_id_type=MESH)

    for t in range(n - 1):
        power_copy(far_first(t, n)).start()
    summed = power_send[...]
    for d in range(1, n):
        power_copy(d).wait_recv()
        summed = summed + power_recv[d]
    total_power = jnp.concatenate([summed] * 16, axis=0).T[0:rhs, 0:1]
    out[...] = residual * lax.rsqrt(total_power * (1.0 / (width * n)) + 1e-6)

    for d in range(1, n):
        coord_copy(d).wait_send()
        value_copy(d).wait_send()
        back_copy(d).wait_send()
        power_copy(d).wait_send()
    for copy in tree_copies:
        copy.wait_send()


def fused_local(n, iterate, target, coords, tree_order, leaf_basis, transfer, coupling):
    rhs, width = iterate.shape
    rank = leaf_basis.shape[1]
    share = width // n
    levels = n.bit_length() - 1
    dma = pltpu.SemaphoreType.DMA
    vmem = pltpu.VMEM
    return pl.pallas_call(
        functools.partial(fused, n, levels),
        out_shape=jax.ShapeDtypeStruct((rhs, width), F32),
        in_specs=[pl.BlockSpec(memory_space=pltpu.HBM)] * 7,
        out_specs=pl.BlockSpec(memory_space=vmem),
        scratch_shapes=[
            vmem(iterate.shape, F32),
            vmem(target.shape, F32),
            vmem(coords.shape, jnp.int32),
            vmem(tree_order.shape, jnp.int32),
            vmem(leaf_basis.shape, BF16),
            vmem(transfer.shape, BF16),
            vmem(coupling.shape, BF16),
            vmem((2 * rhs + 16, width), BF16),
            vmem((16, width), F32),
            vmem((width, width), BF16),
            vmem((n, rhs, share), F32),
            vmem((n, 8, share), F32),
            vmem((rhs, width), F32),
            vmem((8, width), F32),
            vmem((16, width), F32),
            vmem((16, width), F32),
            vmem((width, 16), BF16),
            vmem((width, width), BF16),
            vmem((levels, rhs, rank), F32),
            vmem((n, rhs, rank), F32),
            vmem((n, rhs, share), F32),
            vmem((rhs, width), F32),
            vmem((2 * rhs, width), F32),
            vmem((8, 128), F32),
            vmem((n, 8, 128), F32),
            dma((6,)), dma((n,)),
            dma((n,)), dma((n,)), dma((n,)), dma((n,)),
            dma((n,)), dma((n,)), dma((n,)), dma((n,)), dma((n,)), dma((n,)),
        ],
        compiler_params=pltpu.CompilerParams(
            collective_id=0, has_side_effects=True, vmem_limit_bytes=60 * 2**20
        ),
    )(iterate, target, coords, tree_order, leaf_basis, transfer, coupling)


def swapped(value, axis, stride):
    mask = 2**stride
    pairs = [(source, source ^ mask) for source in range(lax.axis_size(axis))]
    return lax.ppermute(value, axis, pairs)


def product(left, right):
    return jnp.dot(left, right, precision=lax.Precision.HIGHEST)


def matern_block(left_coords, right_coords):
    squared = (left_coords[0][:, None] - right_coords[0][None, :]) ** 2
    squared = squared + (left_coords[1][:, None] - right_coords[1][None, :]) ** 2
    squared = squared + (left_coords[2][:, None] - right_coords[2][None, :]) ** 2
    scaled = jnp.sqrt(3.0 * squared) * 0.0625
    return (1.0 + scaled) * jnp.exp(-scaled)


def near_field(values, points):
    width = values.shape[1]
    block_rows = min(512, width)

    def accumulate(step_number, running):
        offset = step_number * block_rows
        rows_points = lax.dynamic_slice_in_dim(points, offset, block_rows, 1)
        rows_values = lax.dynamic_slice_in_dim(values, offset, block_rows, 1)
        kernel = matern_block(rows_points, points)
        return running + product(rows_values, kernel)

    summed = lax.fori_loop(0, width // block_rows, accumulate, jnp.zeros(values.shape, jnp.float32))
    return 0.0625 * summed


def pair_step(skeleton, height, tables, couplings, final):
    if final:
        payload = skeleton[None]
    else:
        lifted = product(skeleton, tables[height])
        payload = jnp.stack([skeleton, lifted])
    arrived = swapped(payload, "leaf", height)
    coupled_term = product(arrived[0], couplings[height])
    if final:
        return (coupled_term, skeleton)
    return (coupled_term, lifted + arrived[1])


def local(iterate, target, coords, tree_order, leaf_basis, transfer, coupling):
    devices = lax.axis_size("leaf")
    levels_total = devices.bit_length() - 1
    shuffle = tree_order[0]
    outgoing = (iterate[:, shuffle], coords[:, shuffle].astype(jnp.float32))
    tree_values, tree_coords = (
        lax.all_to_all(outgoing[0], "leaf", split_axis=1, concat_axis=1, tiled=True),
        lax.all_to_all(outgoing[1], "leaf", split_axis=1, concat_axis=1, tiled=True),
    )
    nearby = near_field(tree_values, tree_coords)
    skeleton = jnp.dot(
        tree_values.astype(jnp.bfloat16), leaf_basis, preferred_element_type=jnp.float32
    )
    tables = transfer[0].astype(jnp.float32)
    couplings = coupling[0].astype(jnp.float32)
    coupled = []
    for height in range(levels_total):
        coupled_term, skeleton = pair_step(
            skeleton, height, tables, couplings, height == levels_total - 1
        )
        coupled.append(coupled_term)
    downward = coupled[-1]
    for height in range(levels_total - 2, -1, -1):
        lowered = lax.dot_general(
            downward, tables[height], (((1,), (1,)), ((), ())), precision=lax.Precision.HIGHEST
        )
        downward = coupled[height] + lowered
    far_field = lax.dot_general(
        downward.astype(jnp.bfloat16),
        leaf_basis,
        (((1,), (1,)), ((), ())),
        preferred_element_type=jnp.float32,
    )
    applied = nearby + far_field
    returned = lax.all_to_all(applied, "leaf", split_axis=1, concat_axis=1, tiled=True)
    placed = jnp.zeros_like(target).at[:, shuffle].set(returned)
    residual = target - placed
    power = lax.psum(jnp.sum(residual * residual, axis=1), "leaf")
    return residual / jnp.sqrt(power / (target.shape[1] * devices) + 1e-06)[:, None]


def by_shape(iterate, *rest):
    n = lax.axis_size("leaf")
    rhs, width = iterate.shape
    if n & (n - 1) == 0 and n > 1 and width % (128 * n) == 0 and rhs % 16 == 0 and 128 % rhs == 0:
        return fused_local(n, iterate, *rest)
    return local(iterate, *rest)


def solution(mesh):
    placed = (
        P(("group", "rhs"), "leaf"),
        P(("group", "rhs"), "leaf"),
        P(None, ("group", "leaf")),
        P(("group", "leaf"), None),
        P(("group", "leaf"), None),
        P(("group", "leaf"), None, None, None),
        P(("group", "leaf"), None, None, None),
    )
    return jax.shard_map(
        by_shape, mesh=mesh, in_specs=placed, out_specs=P(("group", "rhs"), "leaf"), check_vma=False
    )
```
